32 devices in a mesh: section: 2 (over y), batch: 16 (over z, x, core).
Axes of the slice: x: 2, y: 2, z: 4, core: 2. Of those that a mesh axis runs over, the one named last changes fastest.
Arguments:
- images: bfloat16 [32, 64, 3072], P('batch', None, 'section'), may hold values from -1 to 1
- noise_draw: bfloat16 [32, 64, 3072], P('batch', None, 'section'), may hold values from -6 to 6
- cotangent: bfloat16 [32, 64, 3072], P('batch', None, 'section'), may hold values from -6 to 6
- hue_angle: float32 [32], P('batch'), may hold values from -0.5 to 0.5
- saturation: float32 [32], P('batch'), may hold values from 0.5 to 1.5
- timestep: int32 [32], P('batch'), may hold values from 50 to 199
- stem_weight: bfloat16 [3072, 1024], P('section'), may hold values from -0.109375 to 0.109375
- conv_weight: bfloat16 [2, 9216, 1024], P('section', 'batch'), may hold values from -0.0625 to 0.0625
- emb_weight: bfloat16 [2, 1024, 2048], P('section'), may hold values from -0.1875 to 0.1875
- head_weight: bfloat16 [1024, 3072], P(None, 'section'), may hold values from -0.1875 to 0.1875
Outputs:
- purified: bfloat16 [32, 64, 3072], P('batch', None, 'section')
- colour_grad: float32 [32, 2], P('batch')
The draws below stay inside these ranges and needn't reach their ends.
All inputs are finite; a program needn't handle non-finite values.
Results may differ from the reference program's by a relative error of at most 0.039.
Values may be sent and summed in bfloat16 or wider, within the bound.
A program may use at most 128 MiB of HBM per device.

```python
import math
import jax
import jax.numpy as jnp
from jax import lax

CH = 1024
GROUPS = 32
TEMB = 1024
GRID = 8
TSTEPS = 1000
PV = 3072
SECTIONS = 2
IMAGES = 32


def plant(drawn, stream_key, least, top_value):
    place = [jax.random.randint(jax.random.fold_in(stream_key, axis), (), 0, length) for axis, length in enumerate(drawn.shape)]
    widest = drawn.shape.index(max(drawn.shape))
    neighbour = place[:widest] + [(place[widest] + 1) % drawn.shape[widest]] + place[widest + 1:]
    return drawn.at[tuple(place)].set(least).at[tuple(neighbour)].set(top_value)


def level_of(stream_key, extent, split, low, high):
    level = 1.0
    for position, parts in split:
        steps = jax.random.uniform(jax.random.fold_in(jax.random.fold_in(stream_key, 6), position), (parts,), jnp.float32, low / len(split), high / len(split))
        level = level * jnp.repeat(jnp.exp(steps), extent[position] // parts).reshape((-1,) + (1,) * (len(extent) - 1 - position))
    return level


def gaussian(rng, shape, deviation, reach, shards=(), kind=jnp.bfloat16):
    entries = deviation * jax.random.normal(rng, shape, jnp.float32)
    if shards:
        entries = entries * level_of(rng, shape, shards, -0.22, 0.18)
    return jnp.clip(entries, -reach, reach).astype(kind)


def setup_inputs(seed: int = 0) -> dict:
    keys = jax.random.split(jax.random.key(seed), 11)
    return {
        "images": jnp.clip(jax.random.uniform(keys[0], (IMAGES, GRID * GRID, PV), jnp.float32, -1.0, 1.0) * level_of(keys[0], (IMAGES, GRID * GRID, PV), ((0, 16), (2, 2)), -0.4, 0.0), -1.0, 1.0).astype(jnp.bfloat16),
        "noise_draw": gaussian(keys[1], (IMAGES, GRID * GRID, PV), 1.0, 6.0, ((0, 16), (2, 2))),
        "cotangent": gaussian(keys[2], (IMAGES, GRID * GRID, PV), 1.0, 6.0, ((0, 16), (2, 2))),
        "hue_angle": jnp.clip(jax.random.uniform(keys[3], (IMAGES,), jnp.float32, -0.5, 0.5) * level_of(keys[3], (IMAGES,), ((0, 16),), -0.4, 0.0), -0.5, 0.5),
        "saturation": jnp.clip(0.5 + 1.0 * jax.random.uniform(keys[4], (IMAGES,), jnp.float32) ** level_of(keys[4], (IMAGES,), ((0, 16),), -0.2, 0.2), 0.5, 1.5),
        "timestep": plant(jax.random.randint(keys[5], (IMAGES,), 50, 200), jax.random.fold_in(keys[5], 1), 50, 199).astype(jnp.int32),
        "stem_weight": gaussian(keys[6], (PV, CH), PV ** -0.5, 0.109375, ((0, 2),)),
        "conv_weight": gaussian(keys[7], (SECTIONS, 9 * CH, CH), (9 * CH) ** -0.5, 0.0625, ((0, 2), (1, 16))),
        "emb_weight": gaussian(keys[8], (SECTIONS, TEMB, 2 * CH), TEMB ** -0.5, 0.1875, ((0, 2),)),
        "head_weight": gaussian(keys[9], (CH, PV), CH ** -0.5, 0.1875, ((1, 2),)),
    }


def noise_levels(timestep):
    beta_rates = jnp.linspace(0.0001, 0.02, TSTEPS, dtype=jnp.float32)
    levels = jnp.cumprod(1.0 - beta_rates)
    chosen = jnp.arange(TSTEPS, dtype=jnp.int32)[None, :] == timestep[:, None]
    return lax.optimization_barrier(jnp.sum(jnp.where(chosen, levels[None, :], jnp.float32(0.0)), axis=1))

def time_features(timestep):
    half_width = TEMB // 2
    frequency = jnp.exp(-math.log(10000.0) * jnp.arange(half_width, dtype=jnp.float32) / half_width)
    angles = timestep.astype(jnp.float32)[:, None] * frequency[None, :]
    return jax.nn.silu(jnp.concatenate([jnp.cos(angles), jnp.sin(angles)], axis=1)).astype(jnp.bfloat16)

def colour_maps(hue_angle, saturation):
    grey_map = jnp.full((3, 3), 1.0 / 3.0, dtype=jnp.float32)
    rotate_map = jnp.eye(3, dtype=jnp.float32) - grey_map
    cross_map = jnp.array([[0.0, -1.0, 1.0], [1.0, 0.0, -1.0], [-1.0, 1.0, 0.0]], dtype=jnp.float32) / math.sqrt(3.0)
    cosine = jnp.cos(hue_angle)[:, None, None]
    sine_of = jnp.sin(hue_angle)[:, None, None]
    turning = cosine * rotate_map + sine_of * cross_map
    sat_scale = saturation[:, None, None]
    matrix = grey_map + sat_scale * turning
    hue_slope = sat_scale * (cosine * cross_map - sine_of * rotate_map)
    return (matrix, hue_slope, turning)

def apply_map(matrix, pixels):
    return lax.optimization_barrier(jnp.sum(matrix[:, None, None, :, :] * pixels[:, :, :, None, :], axis=-1))

def conv_branch(feature, weight, scaling):
    number = feature.shape[0]
    channels = feature.shape[2]
    grouped = feature.reshape(number, GRID * GRID, GROUPS, channels // GROUPS)
    centre = lax.optimization_barrier(jnp.mean(grouped, axis=(1, 3), keepdims=True))
    spread_sq = lax.optimization_barrier(jnp.mean(jnp.square(grouped - centre), axis=(1, 3), keepdims=True))
    normed = ((grouped - centre) * lax.rsqrt(spread_sq + 1e-05)).reshape(number, GRID * GRID, channels)
    factor = scaling[:, None, :channels]
    offset = scaling[:, None, channels:]
    active = jax.nn.silu(normed * (1.0 + factor) + offset).astype(jnp.bfloat16)
    padded = jnp.pad(active.reshape(number, GRID, GRID, channels), ((0, 0), (1, 1), (1, 1), (0, 0)))
    taps = [padded[:, row_tap:row_tap + GRID, col_tap:col_tap + GRID, :] for row_tap in range(3) for col_tap in range(3)]
    columns = jnp.concatenate(taps, axis=-1).reshape(number * GRID * GRID, 9 * channels)
    product = jnp.dot(columns, weight, preferred_element_type=jnp.float32)
    return product.reshape(number, GRID * GRID, channels)

def residual_block(feature, weight, scaling):
    primal = feature.astype(jnp.float32)
    return (primal + conv_branch(primal, weight, scaling)).astype(jnp.bfloat16)

def block_adjoint(feature, weight, scaling, upstream):
    primal = feature.astype(jnp.float32)

    def branch_only(probe):
        return conv_branch(probe, weight, scaling)
    _, pullback = jax.vjp(branch_only, primal)
    upstream_f = upstream.astype(jnp.float32)
    return (upstream_f + pullback(upstream_f)[0]).astype(jnp.bfloat16)

def reference(images, noise_draw, cotangent, hue_angle, saturation, timestep, stem_weight, conv_weight, emb_weight, head_weight):
    level = noise_levels(timestep)
    root_level = jnp.sqrt(level)[:, None, None]
    root_noise = jnp.sqrt(1.0 - level)[:, None, None]
    matrix, hue_slope, sat_slope = colour_maps(hue_angle, saturation)
    pixels = images.astype(jnp.float32).reshape(IMAGES, GRID * GRID, PV // 3, 3)
    coloured = apply_map(matrix, pixels).reshape(IMAGES, GRID * GRID, PV)
    noised = root_level * coloured + root_noise * noise_draw.astype(jnp.float32)
    entry_sum = jnp.dot(noised.astype(jnp.bfloat16).reshape(-1, PV), stem_weight, preferred_element_type=jnp.float32)
    feature = entry_sum.astype(jnp.bfloat16).reshape(IMAGES, GRID * GRID, CH)
    embedded = time_features(timestep)
    inputs = []
    offsets = []
    for section_at in range(SECTIONS):
        scaling = jnp.dot(embedded, emb_weight[section_at], preferred_element_type=jnp.float32)
        inputs.append(feature)
        offsets.append(scaling)
        feature = residual_block(feature, conv_weight[section_at], scaling)
    predicted = jnp.dot(feature.reshape(-1, CH), head_weight, preferred_element_type=jnp.float32).reshape(IMAGES, GRID * GRID, PV)
    purified = ((noised - root_noise * predicted) / root_level).astype(jnp.bfloat16)
    weighted = cotangent.astype(jnp.float32) * (1.0 / math.sqrt(GRID * GRID * PV))
    eps_grad = (-(root_noise / root_level) * weighted).astype(jnp.bfloat16)
    adjoint = jnp.dot(eps_grad.reshape(-1, PV), head_weight.T, preferred_element_type=jnp.float32)
    adjoint = adjoint.astype(jnp.bfloat16).reshape(IMAGES, GRID * GRID, CH)
    for section_at in reversed(range(SECTIONS)):
        adjoint = block_adjoint(inputs[section_at], conv_weight[section_at], offsets[section_at], adjoint)
    stem_back = jnp.dot(adjoint.reshape(-1, CH), stem_weight.T, preferred_element_type=jnp.float32).reshape(IMAGES, GRID * GRID, PV)
    pixel_grad = (weighted + root_level * stem_back).reshape(IMAGES, GRID * GRID, PV // 3, 3)
    hue_part = lax.optimization_barrier(jnp.sum(pixel_grad * apply_map(hue_slope, pixels), axis=(1, 2, 3)))
    sat_part = lax.optimization_barrier(jnp.sum(pixel_grad * apply_map(sat_slope, pixels), axis=(1, 2, 3)))
    return (purified, jnp.stack([hue_part, sat_part], axis=1))
```

```python
import math

import jax
import jax.numpy as jnp
from jax import lax
from jax.sharding import PartitionSpec as P

CH = 1024
GROUPS = 32
TEMB = 1024
GRID = 8
TSTEPS = 1000
PV = 3072


def shifted(value, axis, steps):
    count = lax.axis_size(axis)
    pairs = [(source, (source + steps) % count) for source in range(count)]
    return lax.ppermute(value, axis, pairs)


def from_root(block, axis, holder):
    block = jnp.where(lax.axis_index(axis) == holder, block, jnp.zeros_like(block))
    return lax.psum(block, axis)


def noise_levels(timestep):
    beta_rates = jnp.linspace(0.0001, 0.02, TSTEPS, dtype=jnp.float32)
    steps = jnp.arange(TSTEPS, dtype=jnp.int32)[None, :]
    return jnp.prod(jnp.where(steps <= timestep[:, None], 1.0 - beta_rates[None, :], 1.0), axis=1)


def time_features(timestep):
    half_width = TEMB // 2
    frequency = jnp.exp(-math.log(10000.0) * jnp.arange(half_width, dtype=jnp.float32) / half_width)
    angles = timestep.astype(jnp.float32)[:, None] * frequency[None, :]
    return jax.nn.silu(jnp.concatenate([jnp.cos(angles), jnp.sin(angles)], axis=1)).astype(
        jnp.bfloat16
    )


def colour_maps(hue_angle, saturation):
    grey_map = jnp.full((3, 3), 1.0 / 3.0, dtype=jnp.float32)
    rotate_map = jnp.eye(3, dtype=jnp.float32) - grey_map
    cross_map = jnp.array(
        [[0.0, -1.0, 1.0], [1.0, 0.0, -1.0], [-1.0, 1.0, 0.0]], dtype=jnp.float32
    ) / math.sqrt(3.0)
    cosine = jnp.cos(hue_angle)[:, None, None]
    sine_of = jnp.sin(hue_angle)[:, None, None]
    turning = cosine * rotate_map + sine_of * cross_map
    sat_scale = saturation[:, None, None]
    matrix = grey_map + sat_scale * turning
    hue_slope = sat_scale * (cosine * cross_map - sine_of * rotate_map)
    return (matrix, hue_slope, turning)


def apply_map(matrix, pixels):
    return jnp.sum(matrix[:, None, None, :, :] * pixels[:, :, :, None, :], axis=-1)


def conv_branch(feature, weight, scaling):
    number = feature.shape[0]
    channels = feature.shape[2]
    grouped = feature.reshape(number, GRID * GRID, GROUPS, channels // GROUPS)
    centre = jnp.mean(grouped, axis=(1, 3), keepdims=True)
    spread_sq = jnp.mean(jnp.square(grouped - centre), axis=(1, 3), keepdims=True)
    normed = ((grouped - centre) * lax.rsqrt(spread_sq + 1e-05)).reshape(
        number, GRID * GRID, channels
    )
    factor = scaling[:, None, :channels]
    offset = scaling[:, None, channels:]
    active = jax.nn.silu(normed * (1.0 + factor) + offset).astype(jnp.bfloat16)
    padded = jnp.pad(active.reshape(number, GRID, GRID, channels), ((0, 0), (1, 1), (1, 1), (0, 0)))
    taps = [
        padded[:, row_tap : row_tap + GRID, col_tap : col_tap + GRID, :]
        for row_tap in range(3)
        for col_tap in range(3)
    ]
    columns = jnp.concatenate(taps, axis=-1).reshape(number * GRID * GRID, 9 * channels)
    product = jnp.dot(columns, weight, preferred_element_type=jnp.float32)
    return product.reshape(number, GRID * GRID, channels)


def residual_block(feature, weight, scaling):
    primal = feature.astype(jnp.float32)
    return (primal + conv_branch(primal, weight, scaling)).astype(jnp.bfloat16)


def block_adjoint(feature, weight, scaling, upstream):
    primal = feature.astype(jnp.float32)

    def branch_only(probe):
        return conv_branch(probe, weight, scaling)

    _, pullback = jax.vjp(branch_only, primal)
    upstream_f = upstream.astype(jnp.float32)
    return (upstream_f + pullback(upstream_f)[0]).astype(jnp.bfloat16)


def section_total(partial_sum):
    return lax.psum(partial_sum.astype(jnp.bfloat16), "section").astype(jnp.float32)


def send_forward(value):
    return shifted(value, "section", 1)


def send_backward(value):
    return shifted(value, "section", -1)


def spread(value, owner):
    return from_root(value, "section", owner)


def store_one(buffer, value, index_at, is_live):
    previous = lax.dynamic_index_in_dim(buffer, index_at, 0, keepdims=False)
    return lax.dynamic_update_index_in_dim(buffer, jnp.where(is_live, value, previous), index_at, 0)


def run_chain(position, entering, worker, sender):
    number = entering.shape[0]
    clocks = number + lax.axis_size("section") - 1

    def advance(clock, state_in):
        incoming, sources, results = state_in
        member = clock - position
        is_live = (member >= 0) & (member < number)
        index_at = jnp.clip(member, 0, number - 1)
        entry_row = lax.dynamic_index_in_dim(entering, index_at, 0, keepdims=False)
        source = jnp.where(position == 0, entry_row, incoming)

        def run_work():
            return worker(source, index_at)

        def pass_through():
            return source

        result = lax.cond(is_live, run_work, pass_through)
        sources = store_one(sources, source, index_at, is_live)
        results = store_one(results, result, index_at, is_live)
        return (sender(result), sources, results)

    start = (jnp.zeros_like(entering[0]), jnp.zeros_like(entering), jnp.zeros_like(entering))
    final_state = lax.fori_loop(0, clocks, advance, start)
    return (final_state[1], final_state[2])


def local(
    images,
    noise_draw,
    cotangent,
    hue_angle,
    saturation,
    timestep,
    stem_weight,
    conv_weight,
    emb_weight,
    head_weight,
):
    sections = lax.axis_size("section")
    place = lax.axis_index("section")
    number = images.shape[0]
    columns_here = images.shape[2]
    full_conv = lax.all_gather(conv_weight, "batch", axis=1, tiled=True)[0]
    level = noise_levels(timestep)
    root_level = jnp.sqrt(level)[:, None, None]
    root_noise = jnp.sqrt(1.0 - level)[:, None, None]
    matrix, hue_slope, sat_slope = colour_maps(hue_angle, saturation)
    pixels = images.astype(jnp.float32).reshape(number, GRID * GRID, columns_here // 3, 3)
    coloured = apply_map(matrix, pixels).reshape(number, GRID * GRID, columns_here)
    noised = root_level * coloured + root_noise * noise_draw.astype(jnp.float32)
    entry_part = jnp.dot(
        noised.astype(jnp.bfloat16).reshape(-1, columns_here),
        stem_weight,
        preferred_element_type=jnp.float32,
    )
    first = section_total(entry_part).astype(jnp.bfloat16).reshape(number, GRID * GRID, CH)
    offsets = jnp.dot(time_features(timestep), emb_weight[0], preferred_element_type=jnp.float32)

    def forward_work(source, index_at):
        scaling = lax.dynamic_slice_in_dim(offsets, index_at, 1, 0)
        return residual_block(source[None], full_conv, scaling)[0]

    fwd_inputs, fwd_outputs = run_chain(place, first, forward_work, send_forward)
    finals = spread(fwd_outputs, sections - 1)
    predicted = jnp.dot(finals.reshape(-1, CH), head_weight, preferred_element_type=jnp.float32)
    predicted = predicted.reshape(number, GRID * GRID, columns_here)
    purified = ((noised - root_noise * predicted) / root_level).astype(jnp.bfloat16)
    weighted = cotangent.astype(jnp.float32) * (1.0 / math.sqrt(GRID * GRID * PV))
    eps_grad = (-(root_noise / root_level) * weighted).astype(jnp.bfloat16)
    seed_part = lax.dot_general(
        eps_grad.reshape(-1, columns_here),
        head_weight,
        (((1,), (1,)), ((), ())),
        preferred_element_type=jnp.float32,
    )
    seed = section_total(seed_part).astype(jnp.bfloat16).reshape(number, GRID * GRID, CH)

    def adjoint_work(source, index_at):
        saved = lax.dynamic_index_in_dim(fwd_inputs, index_at, 0, keepdims=True)
        scaling = lax.dynamic_slice_in_dim(offsets, index_at, 1, 0)
        return block_adjoint(saved, full_conv, scaling, source[None])[0]

    back_inputs, back_outputs = run_chain(sections - 1 - place, seed, adjoint_work, send_backward)
    grads = spread(back_outputs, 0)
    stem_back = lax.dot_general(
        grads.reshape(-1, CH),
        stem_weight,
        (((1,), (1,)), ((), ())),
        preferred_element_type=jnp.float32,
    )
    stem_back = stem_back.reshape(number, GRID * GRID, columns_here)
    pixel_grad = (weighted + root_level * stem_back).reshape(
        number, GRID * GRID, columns_here // 3, 3
    )
    hue_part = jnp.sum(pixel_grad * apply_map(hue_slope, pixels), axis=(1, 2, 3))
    sat_part = jnp.sum(pixel_grad * apply_map(sat_slope, pixels), axis=(1, 2, 3))
    colour_grad = section_total(jnp.stack([hue_part, sat_part], axis=1))
    return (purified, colour_grad)


def solution(mesh):
    in_specs = (
        P("batch", None, "section"),
        P("batch", None, "section"),
        P("batch", None, "section"),
        P("batch"),
        P("batch"),
        P("batch"),
        P("section", None),
        P("section", "batch", None),
        P("section", None, None),
        P(None, "section"),
    )
    out_specs = (P("batch", None, "section"), P("batch", None))
    return jax.shard_map(local, mesh=mesh, in_specs=in_specs, out_specs=out_specs, check_vma=False)
```

```python
import math

import jax
import jax.numpy as jnp
from jax import lax
from jax.experimental import pallas as pl
from jax.experimental.pallas import tpu as pltpu
from jax.sharding import PartitionSpec as P

CH = 1024
GROUPS = 32
TEMB = 1024
GRID = 8
TSTEPS = 1000
PV = 3072


def noise_levels(timestep):
    beta_rates = jnp.linspace(0.0001, 0.02, TSTEPS, dtype=jnp.float32)
    steps = jnp.arange(TSTEPS, dtype=jnp.int32)[None, :]
    return jnp.prod(jnp.where(steps <= timestep[:, None], 1.0 - beta_rates[None, :], 1.0), axis=1)


def time_features(timestep):
    half_width = TEMB // 2
    frequency = jnp.exp(-math.log(10000.0) * jnp.arange(half_width, dtype=jnp.float32) / half_width)
    angles = timestep.astype(jnp.float32)[:, None] * frequency[None, :]
    return jax.nn.silu(jnp.concatenate([jnp.cos(angles), jnp.sin(angles)], axis=1)).astype(
        jnp.bfloat16
    )


CELLS = GRID * GRID


def circulants(hue_angle, saturation):
    cosine = jnp.cos(hue_angle)
    sine_of = jnp.sin(hue_angle) / math.sqrt(3.0)
    turning = (cosine * (2.0 / 3.0), -cosine / 3.0 - sine_of, -cosine / 3.0 + sine_of)
    matrix = tuple(1.0 / 3.0 + saturation * entry for entry in turning)
    sine_whole = jnp.sin(hue_angle)
    cos_part = cosine / math.sqrt(3.0)
    slope = (
        -sine_whole * (2.0 / 3.0),
        sine_whole / 3.0 - cos_part,
        sine_whole / 3.0 + cos_part,
    )
    return matrix, tuple(saturation * entry for entry in slope), turning


def turned(pixels):
    colour = lax.broadcasted_iota(jnp.int32, (1, 1, pixels.shape[2]), 2) % 3
    after = jnp.where(colour < 2, jnp.roll(pixels, -1, 2), jnp.roll(pixels, 2, 2))
    before = jnp.where(colour > 0, jnp.roll(pixels, 1, 2), jnp.roll(pixels, -2, 2))
    return after, before


def group_mean(total):
    channels = total.shape[1]
    width = channels // GROUPS
    total = jnp.broadcast_to(total, (8, channels))
    lane = lax.broadcasted_iota(jnp.int32, (8, channels), 1)
    step = 1
    while step < width:
        total = total + jnp.where(
            (lane & step) != 0,
            pltpu.roll(total, step, 1),
            pltpu.roll(total, channels - step, 1),
        )
        step *= 2
    return total[0:1] * (1.0 / (CELLS * width))


def normalised(value):
    centred = value - group_mean(jnp.sum(value, axis=0, keepdims=True))
    spread_sq = group_mean(jnp.sum(centred * centred, axis=0, keepdims=True))
    inverse = lax.rsqrt(spread_sq + 1e-05)
    return centred * inverse, inverse


def activate(feature_ref, scaling_ref, act_ref):
    channels = feature_ref.shape[1]
    for image in range(feature_ref.shape[0] // CELLS):
        rows = pl.ds(image * CELLS, CELLS)
        normed, _ = normalised(feature_ref[rows, :].astype(jnp.float32))
        pre = normed * (1.0 + scaling_ref[image : image + 1, :channels])
        pre = pre + scaling_ref[image : image + 1, channels:]
        act_ref[rows, :] = pre * jax.nn.sigmoid(pre)


def branch_back(feature_ref, scaling_ref, image, slope_in):
    channels = feature_ref.shape[1]
    rows = pl.ds(image * CELLS, CELLS)
    normed, inverse = normalised(feature_ref[rows, :].astype(jnp.float32))
    gain = 1.0 + scaling_ref[image : image + 1, :channels]
    pre = normed * gain + scaling_ref[image : image + 1, channels:]
    gate = jax.nn.sigmoid(pre)
    slope = slope_in * (gate * (1.0 + pre * (1.0 - gate))) * gain
    mean_slope = group_mean(jnp.sum(slope, axis=0, keepdims=True))
    mean_cross = group_mean(jnp.sum(slope * normed, axis=0, keepdims=True))
    return inverse * (slope - mean_slope - normed * mean_cross)


def neighbours(values, down, right):
    rows = values.shape[0]
    offset = GRID * down + right
    shifted = pltpu.roll(values, lax.rem(2 * rows - offset, rows), 0)
    row = lax.broadcasted_iota(jnp.int32, (rows, 1), 0)
    high = (row // GRID) % GRID + down
    wide = row % GRID + right
    inside = (high >= 0) & (high < GRID) & (wide >= 0) & (wide < GRID)
    return jnp.where(inside, shifted, 0.0).astype(jnp.bfloat16)


def forward_kernel(feature_ref, scaling_ref, weight_ref, out_ref, act_ref, total_ref):
    tap = pl.program_id(0)

    @pl.when(tap == 0)
    def _():
        activate(feature_ref, scaling_ref, act_ref)
        total_ref[...] = feature_ref[...].astype(jnp.float32)

    columns = neighbours(act_ref[...], tap // 3 - 1, tap % 3 - 1)
    total_ref[...] += jnp.dot(columns, weight_ref[...], preferred_element_type=jnp.float32)

    @pl.when(tap == 8)
    def _():
        out_ref[...] = total_ref[...].astype(jnp.bfloat16)


def add_transposed(tap, upstream_ref, weight_ref, total_ref):
    @pl.when(tap == 0)
    def _():
        total_ref[...] = jnp.zeros_like(total_ref)

    columns = neighbours(upstream_ref[...].astype(jnp.float32), 1 - tap // 3, 1 - tap % 3)
    total_ref[...] += lax.dot_general(
        columns, weight_ref[...], (((1,), (1,)), ((), ())), preferred_element_type=jnp.float32
    )


def transposed_kernel(upstream_ref, weight_ref, out_ref, total_ref):
    tap = pl.program_id(0)
    add_transposed(tap, upstream_ref, weight_ref, total_ref)

    @pl.when(tap == 8)
    def _():
        out_ref[...] = total_ref[...].astype(jnp.bfloat16)


def finish_back(upstream_ref, feature_ref, scaling_ref, slope_ref, out_ref):
    for image in range(upstream_ref.shape[0] // CELLS):
        rows = pl.ds(image * CELLS, CELLS)
        slope_in = slope_ref[rows, :].astype(jnp.bfloat16).astype(jnp.float32)
        grad = branch_back(feature_ref, scaling_ref, image, slope_in)
        out_ref[rows, :] = (upstream_ref[rows, :].astype(jnp.float32) + grad).astype(jnp.bfloat16)


def adjoint_kernel(upstream_ref, feature_ref, scaling_ref, weight_ref, out_ref, total_ref):
    tap = pl.program_id(0)
    add_transposed(tap, upstream_ref, weight_ref, total_ref)

    @pl.when(tap == 8)
    def _():
        finish_back(upstream_ref, feature_ref, scaling_ref, total_ref, out_ref)


def whole(shape):
    return pl.BlockSpec(shape, lambda tap: (0, 0))


def by_tap(kernel, small, weight, scratch):
    rows, channels = small[0].shape
    return pl.pallas_call(
        kernel,
        grid=(9,),
        in_specs=[whole(value.shape) for value in small]
        + [pl.BlockSpec((channels, channels), lambda tap: (tap, 0))],
        out_specs=whole((rows, channels)),
        out_shape=jax.ShapeDtypeStruct((rows, channels), jnp.bfloat16),
        scratch_shapes=[pltpu.VMEM((rows, channels), jnp.float32)] * scratch,
        compiler_params=pltpu.CompilerParams(vmem_limit_bytes=24 * 1024 * 1024),
        cost_estimate=pl.CostEstimate(
            flops=2 * rows * weight.size,
            bytes_accessed=2 * weight.size,
            transcendentals=rows * channels,
        ),
    )(*small, weight)


def forward_block(feature, scaling, weight):
    return by_tap(forward_kernel, (feature, scaling), weight, 2)


def transposed_conv(upstream, weight):
    return by_tap(transposed_kernel, (upstream,), weight, 1)


def adjoint_block(upstream, feature, scaling, weight):
    return by_tap(adjoint_kernel, (upstream, feature, scaling), weight, 1)


def adjoint_from(upstream, feature, scaling, slope_in):
    return pl.pallas_call(
        finish_back,
        out_shape=jax.ShapeDtypeStruct(upstream.shape, jnp.bfloat16),
    )(upstream, feature, scaling, slope_in)


def moved(value, steps):
    count = lax.axis_size("section")
    return lax.ppermute(value, "section", [(at, (at + steps) % count) for at in range(count)])


def section_sum(value):
    if lax.axis_size("section") == 2:
        return value.astype(jnp.float32) + moved(value, 1).astype(jnp.float32)
    return lax.psum(value, "section").astype(jnp.float32)


def two_sections(first, seed, scaling, weight):
    place = lax.axis_index("section")
    early = lax.cond(
        place == 0,
        lambda: forward_block(first, scaling, weight),
        lambda: transposed_conv(seed, weight),
    )
    arrived = moved(early, 1)
    back = moved(adjoint_from(seed, arrived, scaling, early), 1)
    late = lax.cond(
        place == 0,
        lambda: adjoint_block(back, first, scaling, weight),
        lambda: forward_block(arrived, scaling, weight),
    )
    final = jnp.where(place == 0, moved(late, 1), late)
    return final, late


def many_sections(first, seed, scaling, weight):
    sections = lax.axis_size("section")
    place = lax.axis_index("section")
    entering, final = first, first
    current = first
    for at in range(sections):
        entering = jnp.where(place == at, current, entering)
        result = forward_block(current, scaling, weight)
        final = jnp.where(place == at, result, final)
        current = moved(result, 1)
    final = lax.psum(jnp.where(place == sections - 1, final, jnp.zeros_like(final)), "section")
    current = seed
    last = seed
    for at in reversed(range(sections)):
        last = adjoint_block(current, entering, scaling, weight)
        current = moved(last, -1)
    return final, last


def local(
    images,
    noise_draw,
    cotangent,
    hue_angle,
    saturation,
    timestep,
    stem_weight,
    conv_weight,
    emb_weight,
    head_weight,
):
    sections = lax.axis_size("section")
    place = lax.axis_index("section")
    number = images.shape[0]
    columns_here = images.shape[2]
    rows = number * CELLS
    full_conv = lax.all_gather(conv_weight[0], "batch", axis=0, tiled=True)
    level = noise_levels(timestep)
    root_level = jnp.sqrt(level)[:, None, None]
    root_noise = jnp.sqrt(1.0 - level)[:, None, None]
    matrix, hue_slope, sat_slope = circulants(hue_angle, saturation)
    after, before = turned(images)
    variants = [images, after, before]
    wide = [variant.astype(jnp.float32) for variant in variants]
    coloured = sum(entry[:, None, None] * variant for entry, variant in zip(matrix, wide))
    noised = root_level * coloured + root_noise * noise_draw.astype(jnp.float32)
    weighted = cotangent.astype(jnp.float32) * (1.0 / math.sqrt(CELLS * PV))
    eps_grad = (-(root_noise / root_level) * weighted).astype(jnp.bfloat16)
    entry_part = jnp.dot(
        noised.astype(jnp.bfloat16).reshape(rows, columns_here),
        stem_weight,
        preferred_element_type=jnp.float32,
    )
    seed_part = lax.dot_general(
        eps_grad.reshape(rows, columns_here),
        head_weight,
        (((1,), (1,)), ((), ())),
        preferred_element_type=jnp.float32,
    )
    ends = section_sum(jnp.stack([entry_part, seed_part]).astype(jnp.bfloat16))
    ends = ends.astype(jnp.bfloat16)
    scaling = jnp.dot(time_features(timestep), emb_weight[0], preferred_element_type=jnp.float32)
    probes = jnp.dot(
        jnp.stack(variants).reshape(3 * rows, columns_here),
        stem_weight,
        preferred_element_type=jnp.float32,
    )
    probes = section_sum(probes.astype(jnp.bfloat16)).reshape(3, number, CELLS, CH)
    direct = jnp.stack([jnp.sum(weighted * variant, axis=(1, 2)) for variant in wide])
    run = two_sections if sections == 2 else many_sections
    final, adjoint = run(ends[0], ends[1], scaling, full_conv)
    adjoint = adjoint.astype(jnp.float32).reshape(1, number, CELLS, CH)
    through = jnp.sum(adjoint * probes, axis=(2, 3)) * root_level[None, :, 0, 0]
    sums = direct + jnp.where(place == 0, through, 0.0)
    parts = jnp.stack(
        [sum(entry * one for entry, one in zip(slope, sums)) for slope in (hue_slope, sat_slope)],
        axis=1,
    )
    predicted = jnp.dot(final, head_weight, preferred_element_type=jnp.float32)
    predicted = predicted.reshape(number, CELLS, columns_here)
    purified = ((noised - root_noise * predicted) / root_level).astype(jnp.bfloat16)
    return (purified, section_sum(parts))


def solution(mesh):
    in_specs = (
        P("batch", None, "section"),
        P("batch", None, "section"),
        P("batch", None, "section"),
        P("batch"),
        P("batch"),
        P("batch"),
        P("section", None),
        P("section", "batch", None),
        P("section", None, None),
        P(None, "section"),
    )
    out_specs = (P("batch", None, "section"), P("batch", None))
    return jax.shard_map(local, mesh=mesh, in_specs=in_specs, out_specs=out_specs, check_vma=False)
```

```python
import functools
import math

import jax
import jax.numpy as jnp
from jax import lax
from jax.experimental import pallas as pl
from jax.experimental.pallas import tpu as pltpu
from jax.sharding import PartitionSpec as P

CH = 1024
GROUPS = 32
TEMB = 1024
GRID = 8
TSTEPS = 1000
PV = 3072


def noise_levels(timestep):
    beta_rates = jnp.linspace(0.0001, 0.02, TSTEPS, dtype=jnp.float32)
    steps = jnp.arange(TSTEPS, dtype=jnp.int32)[None, :]
    return jnp.prod(jnp.where(steps <= timestep[:, None], 1.0 - beta_rates[None, :], 1.0), axis=1)


def time_features(timestep):
    half_width = TEMB // 2
    frequency = jnp.exp(-math.log(10000.0) * jnp.arange(half_width, dtype=jnp.float32) / half_width)
    angles = timestep.astype(jnp.float32)[:, None] * frequency[None, :]
    return jax.nn.silu(jnp.concatenate([jnp.cos(angles), jnp.sin(angles)], axis=1)).astype(
        jnp.bfloat16
    )


CELLS = GRID * GRID


def circulants(hue_angle, saturation):
    cosine = jnp.cos(hue_angle)
    sine_of = jnp.sin(hue_angle) / math.sqrt(3.0)
    turning = (cosine * (2.0 / 3.0), -cosine / 3.0 - sine_of, -cosine / 3.0 + sine_of)
    matrix = tuple(1.0 / 3.0 + saturation * entry for entry in turning)
    sine_whole = jnp.sin(hue_angle)
    cos_part = cosine / math.sqrt(3.0)
    slope = (
        -sine_whole * (2.0 / 3.0),
        sine_whole / 3.0 - cos_part,
        sine_whole / 3.0 + cos_part,
    )
    return matrix, tuple(saturation * entry for entry in slope), turning


def turned(pixels):
    colour = lax.broadcasted_iota(jnp.int32, (1, 1, pixels.shape[2]), 2) % 3
    after = jnp.where(colour < 2, jnp.roll(pixels, -1, 2), jnp.roll(pixels, 2, 2))
    before = jnp.where(colour > 0, jnp.roll(pixels, 1, 2), jnp.roll(pixels, -2, 2))
    return after, before


def group_mean(total):
    channels = total.shape[1]
    width = channels // GROUPS
    total = jnp.broadcast_to(total, (8, channels))
    lane = lax.broadcasted_iota(jnp.int32, (8, channels), 1)
    step = 1
    while step < width:
        total = total + jnp.where(
            (lane & step) != 0,
            pltpu.roll(total, step, 1),
            pltpu.roll(total, channels - step, 1),
        )
        step *= 2
    return total[0:1] * (1.0 / (CELLS * width))


def normalised(value):
    centred = value - group_mean(jnp.sum(value, axis=0, keepdims=True))
    spread_sq = group_mean(jnp.sum(centred * centred, axis=0, keepdims=True))
    inverse = lax.rsqrt(spread_sq + 1e-05)
    return centred * inverse, inverse


def activate(feature_ref, scaling_ref, act_ref):
    channels = feature_ref.shape[1]
    for image in range(feature_ref.shape[0] // CELLS):
        rows = pl.ds(image * CELLS, CELLS)
        normed, _ = normalised(feature_ref[rows, :].astype(jnp.float32))
        pre = normed * (1.0 + scaling_ref[image : image + 1, :channels])
        pre = pre + scaling_ref[image : image + 1, channels:]
        act_ref[rows, :] = pre * jax.nn.sigmoid(pre)


def branch_back(feature_ref, scaling_ref, image, slope_in):
    channels = feature_ref.shape[1]
    rows = pl.ds(image * CELLS, CELLS)
    normed, inverse = normalised(feature_ref[rows, :].astype(jnp.float32))
    gain = 1.0 + scaling_ref[image : image + 1, :channels]
    pre = normed * gain + scaling_ref[image : image + 1, channels:]
    gate = jax.nn.sigmoid(pre)
    slope = slope_in * (gate * (1.0 + pre * (1.0 - gate))) * gain
    mean_slope = group_mean(jnp.sum(slope, axis=0, keepdims=True))
    mean_cross = group_mean(jnp.sum(slope * normed, axis=0, keepdims=True))
    return inverse * (slope - mean_slope - normed * mean_cross)


def neighbours(values, down, right):
    rows = values.shape[0]
    offset = GRID * down + right
    shifted = pltpu.roll(values, lax.rem(2 * rows - offset, rows), 0)
    row = lax.broadcasted_iota(jnp.int32, (rows, 1), 0)
    high = (row // GRID) % GRID + down
    wide = row % GRID + right
    inside = (high >= 0) & (high < GRID) & (wide >= 0) & (wide < GRID)
    return jnp.where(inside, shifted, 0.0).astype(jnp.bfloat16)


TAPS = 3


def column_slices(weight_refs, begin=0):
    for ref in weight_refs:
        yield ref, pl.ds(begin, ref.shape[1])
        begin += ref.shape[1]


def add_forward(step, begin, act_ref, weight_refs, total_ref):
    channels = act_ref.shape[1]
    values = act_ref[...]
    for right in range(TAPS):
        columns = neighbours(values, step - 1, right - 1)
        taken = pl.ds(right * channels, channels)
        for ref, here in column_slices(weight_refs):
            total_ref[:, here] += jnp.dot(
                columns, ref[taken, :], preferred_element_type=jnp.float32
            )


def forward_kernel(begin, feature_ref, scaling_ref, *refs):
    *weight_refs, out_ref, act_ref, total_ref = refs
    step = pl.program_id(0)

    @pl.when(step == 0)
    def _():
        activate(feature_ref, scaling_ref, act_ref)
        here = pl.ds(begin, total_ref.shape[1])
        total_ref[...] = feature_ref[:, here].astype(jnp.float32)

    add_forward(step, begin, act_ref, weight_refs, total_ref)

    @pl.when(step == TAPS - 1)
    def _():
        out_ref[...] = total_ref[...].astype(jnp.bfloat16)


def add_transposed(step, begin, upstream_ref, weight_refs, total_ref):
    channels = upstream_ref.shape[1]
    values = upstream_ref[...].astype(jnp.float32)
    for right in range(TAPS):
        taken = pl.ds(right * channels, channels)
        for ref, here in column_slices(weight_refs, begin):
            columns = neighbours(values[:, here.start : here.start + here.size], 1 - step, 1 - right)
            total_ref[...] += lax.dot_general(
                columns,
                ref[taken, :],
                (((1,), (1,)), ((), ())),
                preferred_element_type=jnp.float32,
            )


def transposed_kernel(begin, upstream_ref, before_ref, *refs):
    *weight_refs, total_ref = refs
    step = pl.program_id(0)

    @pl.when(step == 0)
    def _():
        total_ref[...] = before_ref[...]

    add_transposed(step, begin, upstream_ref, weight_refs, total_ref)


def finish_back(upstream_ref, feature_ref, scaling_ref, slope_ref, out_ref):
    for image in range(upstream_ref.shape[0] // CELLS):
        rows = pl.ds(image * CELLS, CELLS)
        slope_in = slope_ref[rows, :].astype(jnp.bfloat16).astype(jnp.float32)
        grad = branch_back(feature_ref, scaling_ref, image, slope_in)
        out_ref[rows, :] = (upstream_ref[rows, :].astype(jnp.float32) + grad).astype(jnp.bfloat16)


def adjoint_kernel(upstream_ref, feature_ref, scaling_ref, *refs):
    *weight_refs, out_ref, total_ref = refs
    step = pl.program_id(0)

    @pl.when(step == 0)
    def _():
        total_ref[...] = jnp.zeros_like(total_ref)

    add_transposed(step, 0, upstream_ref, weight_refs, total_ref)

    @pl.when(step == TAPS - 1)
    def _():
        finish_back(upstream_ref, feature_ref, scaling_ref, total_ref, out_ref)


def whole(shape):
    return pl.BlockSpec(shape, lambda step: (0, 0))


def by_tap(kernel, small, weights, width, kind, scratch):
    rows, channels = small[0].shape
    size = sum(weight.size for weight in weights)
    return pl.pallas_call(
        kernel,
        grid=(TAPS,),
        in_specs=[whole(value.shape) for value in small]
        + [
            pl.BlockSpec((TAPS * channels, weight.shape[1]), lambda step: (step, 0))
            for weight in weights
        ],
        out_specs=whole((rows, width)),
        out_shape=jax.ShapeDtypeStruct((rows, width), kind),
        scratch_shapes=[pltpu.VMEM((rows, across), jnp.float32) for across in scratch],
        compiler_params=pltpu.CompilerParams(vmem_limit_bytes=32 * 1024 * 1024),
        cost_estimate=pl.CostEstimate(
            flops=2 * rows * size, bytes_accessed=2 * size, transcendentals=rows * channels
        ),
    )(*small, *weights)


def forward_block(feature, scaling, weights, begin=0):
    width = sum(weight.shape[1] for weight in weights)
    kernel = functools.partial(forward_kernel, begin)
    scratch = (feature.shape[1], width)
    return by_tap(kernel, (feature, scaling), weights, width, jnp.bfloat16, scratch)


def transposed_conv(upstream, before, weights, begin):
    kernel = functools.partial(transposed_kernel, begin)
    return by_tap(kernel, (upstream, before), weights, upstream.shape[1], jnp.float32, ())


def adjoint_block(upstream, feature, scaling, weights):
    width = upstream.shape[1]
    small = (upstream, feature, scaling)
    return by_tap(adjoint_kernel, small, weights, width, jnp.bfloat16, (width,))


def adjoint_from(upstream, feature, scaling, slope_in):
    return pl.pallas_call(
        finish_back,
        out_shape=jax.ShapeDtypeStruct(upstream.shape, jnp.bfloat16),
    )(upstream, feature, scaling, slope_in)


def moved(value, steps):
    count = lax.axis_size("section")
    return lax.ppermute(value, "section", [(at, (at + steps) % count) for at in range(count)])


def section_sum(value):
    if lax.axis_size("section") == 2:
        return value.astype(jnp.float32) + moved(value, 1).astype(jnp.float32)
    return lax.psum(value, "section").astype(jnp.float32)


def two_sections(first, seed, scaling, weights):
    place = lax.axis_index("section")
    pieces = []
    slope = jnp.zeros(seed.shape, jnp.float32)
    begin = 0
    for part in weights:

        def ahead(part=part, slope=slope, begin=begin):
            return forward_block(first, scaling, (part,), begin), slope

        def behind(part=part, slope=slope, begin=begin):
            other = jnp.zeros((seed.shape[0], part.shape[1]), jnp.bfloat16)
            return other, transposed_conv(seed, slope, (part,), begin)

        piece, slope = lax.cond(place == 0, ahead, behind)
        pieces.append(moved(piece, 1))
        begin += part.shape[1]
    arrived = jnp.concatenate(pieces, axis=1)
    back = moved(adjoint_from(seed, arrived, scaling, slope), 1)
    late = lax.cond(
        place == 0,
        lambda: adjoint_block(back, first, scaling, weights),
        lambda: forward_block(arrived, scaling, weights),
    )
    final = jnp.where(place == 0, moved(late, 1), late)
    return final, late


def many_sections(first, seed, scaling, weights):
    sections = lax.axis_size("section")
    place = lax.axis_index("section")
    entering, final = first, first
    current = first
    for at in range(sections):
        entering = jnp.where(place == at, current, entering)
        result = forward_block(current, scaling, weights)
        final = jnp.where(place == at, result, final)
        current = moved(result, 1)
    final = lax.psum(jnp.where(place == sections - 1, final, jnp.zeros_like(final)), "section")
    current = seed
    last = seed
    for at in reversed(range(sections)):
        last = adjoint_block(current, entering, scaling, weights)
        current = moved(last, -1)
    return final, last


def local(
    images,
    noise_draw,
    cotangent,
    hue_angle,
    saturation,
    timestep,
    stem_weight,
    conv_weight,
    emb_weight,
    head_weight,
):
    sections = lax.axis_size("section")
    place = lax.axis_index("section")
    number = images.shape[0]
    columns_here = images.shape[2]
    rows = number * CELLS
    half = CH // 2
    full_conv = tuple(
        lax.all_gather(conv_weight[0, :, begin : begin + half], "batch", axis=0, tiled=True)
        for begin in (0, half)
    )
    level = noise_levels(timestep)
    root_level = jnp.sqrt(level)[:, None, None]
    root_noise = jnp.sqrt(1.0 - level)[:, None, None]
    matrix, hue_slope, sat_slope = circulants(hue_angle, saturation)
    after, before = turned(images)
    variants = [images, after, before]
    wide = [variant.astype(jnp.float32) for variant in variants]
    coloured = sum(entry[:, None, None] * variant for entry, variant in zip(matrix, wide))
    noised = root_level * coloured + root_noise * noise_draw.astype(jnp.float32)
    weighted = cotangent.astype(jnp.float32) * (1.0 / math.sqrt(CELLS * PV))
    eps_grad = (-(root_noise / root_level) * weighted).astype(jnp.bfloat16)
    entry_part = jnp.dot(
        noised.astype(jnp.bfloat16).reshape(rows, columns_here),
        stem_weight,
        preferred_element_type=jnp.float32,
    )
    seed_part = lax.dot_general(
        eps_grad.reshape(rows, columns_here),
        head_weight,
        (((1,), (1,)), ((), ())),
        preferred_element_type=jnp.float32,
    )
    ends = section_sum(jnp.stack([entry_part, seed_part]).astype(jnp.bfloat16))
    ends = ends.astype(jnp.bfloat16)
    scaling = jnp.dot(time_features(timestep), emb_weight[0], preferred_element_type=jnp.float32)
    probes = jnp.dot(
        jnp.stack(variants).reshape(3 * rows, columns_here),
        stem_weight,
        preferred_element_type=jnp.float32,
    )
    probes = section_sum(probes.astype(jnp.bfloat16)).reshape(3, number, CELLS, CH)
    direct = jnp.stack([jnp.sum(weighted * variant, axis=(1, 2)) for variant in wide])
    run = two_sections if sections == 2 else many_sections
    final, adjoint = run(ends[0], ends[1], scaling, full_conv)
    adjoint = adjoint.astype(jnp.float32).reshape(1, number, CELLS, CH)
    through = jnp.sum(adjoint * probes, axis=(2, 3)) * root_level[None, :, 0, 0]
    sums = direct + jnp.where(place == 0, through, 0.0)
    parts = jnp.stack(
        [sum(entry * one for entry, one in zip(slope, sums)) for slope in (hue_slope, sat_slope)],
        axis=1,
    )
    predicted = jnp.dot(final, head_weight, preferred_element_type=jnp.float32)
    predicted = predicted.reshape(number, CELLS, columns_here)
    purified = ((noised - root_noise * predicted) / root_level).astype(jnp.bfloat16)
    return (purified, section_sum(parts))


def solution(mesh):
    in_specs = (
        P("batch", None, "section"),
        P("batch", None, "section"),
        P("batch", None, "section"),
        P("batch"),
        P("batch"),
        P("batch"),
        P("section", None),
        P("section", "batch", None),
        P("section", None, None),
        P(None, "section"),
    )
    out_specs = (P("batch", None, "section"), P("batch", None))
    return jax.shard_map(local, mesh=mesh, in_specs=in_specs, out_specs=out_specs, check_vma=False)
```

```python
import math

import jax
import jax.numpy as jnp
from jax import lax
from jax.experimental import pallas as pl
from jax.experimental.pallas import tpu as pltpu
from jax.sharding import PartitionSpec as P

CH = 1024
GROUPS = 32
TEMB = 1024
GRID = 8
TSTEPS = 1000
PV = 3072


def noise_levels(timestep):
    beta_rates = jnp.linspace(0.0001, 0.02, TSTEPS, dtype=jnp.float32)
    steps = jnp.arange(TSTEPS, dtype=jnp.int32)[None, :]
    return jnp.prod(jnp.where(steps <= timestep[:, None], 1.0 - beta_rates[None, :], 1.0), axis=1)


def time_features(timestep):
    half_width = TEMB // 2
    frequency = jnp.exp(-math.log(10000.0) * jnp.arange(half_width, dtype=jnp.float32) / half_width)
    angles = timestep.astype(jnp.float32)[:, None] * frequency[None, :]
    return jax.nn.silu(jnp.concatenate([jnp.cos(angles), jnp.sin(angles)], axis=1)).astype(
        jnp.bfloat16
    )


CELLS = GRID * GRID


def circulants(hue_angle, saturation):
    cosine = jnp.cos(hue_angle)
    sine_of = jnp.sin(hue_angle) / math.sqrt(3.0)
    turning = (cosine * (2.0 / 3.0), -cosine / 3.0 - sine_of, -cosine / 3.0 + sine_of)
    matrix = tuple(1.0 / 3.0 + saturation * entry for entry in turning)
    sine_whole = jnp.sin(hue_angle)
    cos_part = cosine / math.sqrt(3.0)
    slope = (
        -sine_whole * (2.0 / 3.0),
        sine_whole / 3.0 - cos_part,
        sine_whole / 3.0 + cos_part,
    )
    return matrix, tuple(saturation * entry for entry in slope), turning


def turned(pixels):
    colour = lax.broadcasted_iota(jnp.int32, (1, 1, pixels.shape[2]), 2) % 3
    after = jnp.where(colour < 2, jnp.roll(pixels, -1, 2), jnp.roll(pixels, 2, 2))
    before = jnp.where(colour > 0, jnp.roll(pixels, 1, 2), jnp.roll(pixels, -2, 2))
    return after, before


def group_mean(total):
    channels = total.shape[1]
    width = channels // GROUPS
    total = jnp.broadcast_to(total, (8, channels))
    lane = lax.broadcasted_iota(jnp.int32, (8, channels), 1)
    step = 1
    while step < width:
        total = total + jnp.where(
            (lane & step) != 0,
            pltpu.roll(total, step, 1),
            pltpu.roll(total, channels - step, 1),
        )
        step *= 2
    return total[0:1] * (1.0 / (CELLS * width))


def normalised(value):
    centred = value - group_mean(jnp.sum(value, axis=0, keepdims=True))
    spread_sq = group_mean(jnp.sum(centred * centred, axis=0, keepdims=True))
    inverse = lax.rsqrt(spread_sq + 1e-05)
    return centred * inverse, inverse


def activate(feature_ref, scaling_ref, act_ref):
    channels = feature_ref.shape[1]
    for image in range(feature_ref.shape[0] // CELLS):
        rows = pl.ds(image * CELLS, CELLS)
        normed, _ = normalised(feature_ref[rows, :].astype(jnp.float32))
        pre = normed * (1.0 + scaling_ref[image : image + 1, :channels])
        pre = pre + scaling_ref[image : image + 1, channels:]
        act_ref[rows, :] = pre * jax.nn.sigmoid(pre)


def branch_back(feature_ref, scaling_ref, image, slope_in):
    channels = feature_ref.shape[1]
    rows = pl.ds(image * CELLS, CELLS)
    normed, inverse = normalised(feature_ref[rows, :].astype(jnp.float32))
    gain = 1.0 + scaling_ref[image : image + 1, :channels]
    pre = normed * gain + scaling_ref[image : image + 1, channels:]
    gate = jax.nn.sigmoid(pre)
    slope = slope_in * (gate * (1.0 + pre * (1.0 - gate))) * gain
    mean_slope = group_mean(jnp.sum(slope, axis=0, keepdims=True))
    mean_cross = group_mean(jnp.sum(slope * normed, axis=0, keepdims=True))
    return inverse * (slope - mean_slope - normed * mean_cross)


def neighbours(values, down, right):
    rows = values.shape[0]
    offset = GRID * down + right
    shifted = pltpu.roll(values, lax.rem(2 * rows - offset, rows), 0)
    row = lax.broadcasted_iota(jnp.int32, (rows, 1), 0)
    high = (row // GRID) % GRID + down
    wide = row % GRID + right
    inside = (high >= 0) & (high < GRID) & (wide >= 0) & (wide < GRID)
    return jnp.where(inside, shifted, 0.0).astype(jnp.bfloat16)


TAPS = 3


def column_slices(weight_refs):
    begin = 0
    for ref in weight_refs:
        yield ref, pl.ds(begin, ref.shape[1])
        begin += ref.shape[1]


def add_forward(step, act_ref, weight_refs, total_ref):
    channels = act_ref.shape[1]
    values = act_ref[...]
    for right in range(TAPS):
        columns = neighbours(values, step - 1, right - 1)
        taken = pl.ds(right * channels, channels)
        for ref, here in column_slices(weight_refs):
            total_ref[:, here] += jnp.dot(
                columns, ref[taken, :], preferred_element_type=jnp.float32
            )


def forward_kernel(feature_ref, scaling_ref, *refs):
    *weight_refs, out_ref, act_ref, total_ref = refs
    step = pl.program_id(0)

    @pl.when(step == 0)
    def _():
        activate(feature_ref, scaling_ref, act_ref)
        total_ref[...] = feature_ref[...].astype(jnp.float32)

    add_forward(step, act_ref, weight_refs, total_ref)

    @pl.when(step == TAPS - 1)
    def _():
        out_ref[...] = total_ref[...].astype(jnp.bfloat16)


def add_transposed(step, upstream_ref, weight_refs, total_ref):
    channels = upstream_ref.shape[1]
    values = upstream_ref[...].astype(jnp.float32)
    for right in range(TAPS):
        taken = pl.ds(right * channels, channels)
        for ref, here in column_slices(weight_refs):
            columns = neighbours(values[:, here.start : here.start + here.size], 1 - step, 1 - right)
            total_ref[...] += lax.dot_general(
                columns,
                ref[taken, :],
                (((1,), (1,)), ((), ())),
                preferred_element_type=jnp.float32,
            )


def transposed_kernel(upstream_ref, *refs):
    *weight_refs, out_ref, total_ref = refs
    step = pl.program_id(0)

    @pl.when(step == 0)
    def _():
        total_ref[...] = jnp.zeros_like(total_ref)

    add_transposed(step, upstream_ref, weight_refs, total_ref)

    @pl.when(step == TAPS - 1)
    def _():
        out_ref[...] = total_ref[...].astype(jnp.bfloat16)


def finish_back(upstream_ref, feature_ref, scaling_ref, slope_ref, out_ref):
    for image in range(upstream_ref.shape[0] // CELLS):
        rows = pl.ds(image * CELLS, CELLS)
        slope_in = slope_ref[rows, :].astype(jnp.bfloat16).astype(jnp.float32)
        grad = branch_back(feature_ref, scaling_ref, image, slope_in)
        out_ref[rows, :] = (upstream_ref[rows, :].astype(jnp.float32) + grad).astype(jnp.bfloat16)


def adjoint_kernel(upstream_ref, feature_ref, scaling_ref, *refs):
    *weight_refs, out_ref, total_ref = refs
    step = pl.program_id(0)

    @pl.when(step == 0)
    def _():
        total_ref[...] = jnp.zeros_like(total_ref)

    add_transposed(step, upstream_ref, weight_refs, total_ref)

    @pl.when(step == TAPS - 1)
    def _():
        finish_back(upstream_ref, feature_ref, scaling_ref, total_ref, out_ref)


def whole(shape):
    return pl.BlockSpec(shape, lambda step: (0, 0))


def by_tap(kernel, small, weights, width, kind, scratch):
    rows, channels = small[0].shape
    size = sum(weight.size for weight in weights)
    return pl.pallas_call(
        kernel,
        grid=(TAPS,),
        in_specs=[whole(value.shape) for value in small]
        + [
            pl.BlockSpec((TAPS * channels, weight.shape[1]), lambda step: (step, 0))
            for weight in weights
        ],
        out_specs=whole((rows, width)),
        out_shape=jax.ShapeDtypeStruct((rows, width), kind),
        scratch_shapes=[pltpu.VMEM((rows, across), jnp.float32) for across in scratch],
        compiler_params=pltpu.CompilerParams(vmem_limit_bytes=32 * 1024 * 1024),
        cost_estimate=pl.CostEstimate(
            flops=2 * rows * size, bytes_accessed=2 * size, transcendentals=rows * channels
        ),
    )(*small, *weights)


def forward_block(feature, scaling, weights):
    width = feature.shape[1]
    return by_tap(forward_kernel, (feature, scaling), weights, width, jnp.bfloat16, (width, width))


def transposed_conv(upstream, weights):
    width = upstream.shape[1]
    return by_tap(transposed_kernel, (upstream,), weights, width, jnp.bfloat16, (width,))


def adjoint_block(upstream, feature, scaling, weights):
    width = upstream.shape[1]
    small = (upstream, feature, scaling)
    return by_tap(adjoint_kernel, small, weights, width, jnp.bfloat16, (width,))


def adjoint_from(upstream, feature, scaling, slope_in):
    return pl.pallas_call(
        finish_back,
        out_shape=jax.ShapeDtypeStruct(upstream.shape, jnp.bfloat16),
    )(upstream, feature, scaling, slope_in)


def moved(value, steps):
    count = lax.axis_size("section")
    return lax.ppermute(value, "section", [(at, (at + steps) % count) for at in range(count)])


def section_sum(value):
    if lax.axis_size("section") == 2:
        return value.astype(jnp.float32) + moved(value, 1).astype(jnp.float32)
    return lax.psum(value, "section").astype(jnp.float32)


def two_sections(first, seed, scaling, weights):
    place = lax.axis_index("section")
    early = lax.cond(
        place == 0,
        lambda: forward_block(first, scaling, weights),
        lambda: transposed_conv(seed, weights),
    )
    arrived = moved(early, 1)
    back = moved(adjoint_from(seed, arrived, scaling, early), 1)
    late = lax.cond(
        place == 0,
        lambda: adjoint_block(back, first, scaling, weights),
        lambda: forward_block(arrived, scaling, weights),
    )
    final = jnp.where(place == 0, moved(late, 1), late)
    return final, late


def many_sections(first, seed, scaling, weights):
    sections = lax.axis_size("section")
    place = lax.axis_index("section")
    entering, final = first, first
    current = first
    for at in range(sections):
        entering = jnp.where(place == at, current, entering)
        result = forward_block(current, scaling, weights)
        final = jnp.where(place == at, result, final)
        current = moved(result, 1)
    final = lax.psum(jnp.where(place == sections - 1, final, jnp.zeros_like(final)), "section")
    current = seed
    last = seed
    for at in reversed(range(sections)):
        last = adjoint_block(current, entering, scaling, weights)
        current = moved(last, -1)
    return final, last


def local(
    images,
    noise_draw,
    cotangent,
    hue_angle,
    saturation,
    timestep,
    stem_weight,
    conv_weight,
    emb_weight,
    head_weight,
):
    sections = lax.axis_size("section")
    place = lax.axis_index("section")
    number = images.shape[0]
    columns_here = images.shape[2]
    rows = number * CELLS
    full_conv = (lax.all_gather(conv_weight[0], "batch", axis=0, tiled=True),)
    level = noise_levels(timestep)
    root_level = jnp.sqrt(level)[:, None, None]
    root_noise = jnp.sqrt(1.0 - level)[:, None, None]
    matrix, hue_slope, sat_slope = circulants(hue_angle, saturation)
    after, before = turned(images)
    variants = [images, after, before]
    wide = [variant.astype(jnp.float32) for variant in variants]
    coloured = sum(entry[:, None, None] * variant for entry, variant in zip(matrix, wide))
    noised = root_level * coloured + root_noise * noise_draw.astype(jnp.float32)
    weighted = cotangent.astype(jnp.float32) * (1.0 / math.sqrt(CELLS * PV))
    eps_grad = (-(root_noise / root_level) * weighted).astype(jnp.bfloat16)
    entry_part = jnp.dot(
        noised.astype(jnp.bfloat16).reshape(rows, columns_here),
        stem_weight,
        preferred_element_type=jnp.float32,
    )
    seed_part = lax.dot_general(
        eps_grad.reshape(rows, columns_here),
        head_weight,
        (((1,), (1,)), ((), ())),
        preferred_element_type=jnp.float32,
    )
    ends = section_sum(jnp.stack([entry_part, seed_part]).astype(jnp.bfloat16))
    ends = ends.astype(jnp.bfloat16)
    scaling = jnp.dot(time_features(timestep), emb_weight[0], preferred_element_type=jnp.float32)
    probes = jnp.dot(
        jnp.stack(variants).reshape(3 * rows, columns_here),
        stem_weight,
        preferred_element_type=jnp.float32,
    )
    probes = section_sum(probes.astype(jnp.bfloat16)).reshape(3, number, CELLS, CH)
    direct = jnp.stack([jnp.sum(weighted * variant, axis=(1, 2)) for variant in wide])
    run = two_sections if sections == 2 else many_sections
    final, adjoint = run(ends[0], ends[1], scaling, full_conv)
    adjoint = adjoint.astype(jnp.float32).reshape(1, number, CELLS, CH)
    through = jnp.sum(adjoint * probes, axis=(2, 3)) * root_level[None, :, 0, 0]
    sums = direct + jnp.where(place == 0, through, 0.0)
    parts = jnp.stack(
        [sum(entry * one for entry, one in zip(slope, sums)) for slope in (hue_slope, sat_slope)],
        axis=1,
    )
    predicted = jnp.dot(final, head_weight, preferred_element_type=jnp.float32)
    predicted = predicted.reshape(number, CELLS, columns_here)
    purified = ((noised - root_noise * predicted) / root_level).astype(jnp.bfloat16)
    return (purified, section_sum(parts))


def solution(mesh):
    in_specs = (
        P("batch", None, "section"),
        P("batch", None, "section"),
        P("batch", None, "section"),
        P("batch"),
        P("batch"),
        P("batch"),
        P("section", None),
        P("section", "batch", None),
        P("section", None, None),
        P(None, "section"),
    )
    out_specs = (P("batch", None, "section"), P("batch", None))
    return jax.shard_map(local, mesh=mesh, in_specs=in_specs, out_specs=out_specs, check_vma=False)
```
